32 devices in a mesh: slab: 8 (over y, x, core), field: 4 (over z).
Axes of the slice: x: 2, y: 2, z: 4, core: 2. Of those that a mesh axis runs over, the one named last changes fastest.
Arguments:
- snaps: bfloat16 [4, 16, 3, 32, 2048], P('field', 'slab'), may hold values from -6 to 6
- writer_map: int32 [64], replicated, may hold values from 0 to 63, each once
- omega: int32 [64, 64], replicated, may hold values from -3 to 3
- face_level: int32 [32], replicated, may hold values from 0 to 11
Outputs:
- sketch_rows: float32 [4, 16, 64], P('field')
- core: float32 [64, 64], replicated
The draws below stay inside these ranges and needn't reach their ends.
All inputs are finite; a program needn't handle non-finite values.
Results may differ from the reference program's by a relative error of at most 0.00035.
Values may be sent and summed in bfloat16 or wider, within the bound.
A program may use at most 128 MiB of HBM per device.

```python
import jax
import jax.numpy as jnp
from jax import lax

P_SIZE = 2048
SKETCH = 64
COMP = 3
LEVELS = 12
WRITERS = 4
SNAPG = 16
SNAPS = 64
NY = 32


def set_ends(drawn, rng, low, high):
    dims = drawn.shape
    place = [jax.random.randint(jax.random.fold_in(rng, axis), (), 0, dims[axis]) for axis in range(len(dims))]
    drawn = drawn.at[tuple(place)].set(low)
    longest = dims.index(max(dims))
    place[longest] = (place[longest] + 1) % dims[longest]
    return drawn.at[tuple(place)].set(high)


def block_scale(key, extent, split, least, high):
    level = 1.0
    for dim, parts in split:
        draws = jax.random.uniform(jax.random.fold_in(jax.random.fold_in(key, 6), dim), (parts,), jnp.float32, least / len(split), high / len(split))
        level = level * jnp.repeat(jnp.exp(draws), extent[dim] // parts).reshape((-1,) + (1,) * (len(extent) - 1 - dim))
    return level


def centred(key, shape, spread, most, shards=(), held_as=jnp.bfloat16):
    drawn = jax.random.normal(key, shape, jnp.float32) * spread
    if len(shards) > 0:
        drawn = block_scale(key, shape, shards, -0.22, 0.18) * drawn
    return jnp.clip(drawn, min=-most, max=most).astype(held_as)


def setup_inputs(seed: int = 0) -> dict:
    key_list = jax.random.split(jax.random.key(seed), 5)
    snaps = centred(key_list[0], (WRITERS, SNAPG, COMP, NY, P_SIZE), 1.0, 6.0, ((0, 4), (1, 8)))
    writer_map = jax.random.permutation(key_list[1], SNAPS).astype(jnp.int32)
    omega = set_ends(jax.random.randint(key_list[2], (SNAPS, SKETCH), -3, 4), jax.random.fold_in(key_list[2], 1), -3, 3).astype(jnp.int32)
    face_level = set_ends(jax.random.randint(key_list[3], (NY,), 0, LEVELS), jax.random.fold_in(key_list[3], 1), 0, LEVELS - 1).astype(jnp.int32)
    return {"snaps": snaps, "writer_map": writer_map, "omega": omega, "face_level": face_level}


def reference(snaps, writer_map, omega, face_level):
    test = omega[writer_map].astype(jnp.bfloat16)
    dy = 0.5 * jnp.power(jnp.float32(1.12), face_level.astype(jnp.float32))
    weight = dy.reshape(1, 1, NY, 1)
    coupling = (1.0 / dy).reshape(1, 1, NY, 1)
    flat = snaps.reshape(SNAPS, COMP * NY * P_SIZE)
    sketched = jnp.dot(test.T, flat, preferred_element_type=jnp.float32).reshape(SKETCH, COMP, NY, P_SIZE)
    below = jnp.concatenate([jnp.zeros((SKETCH, COMP, 1, P_SIZE), jnp.float32), sketched[:, :, :-1]], axis=2)
    flux = coupling * (sketched - below)
    above = jnp.concatenate([flux[:, :, 1:], jnp.zeros((SKETCH, COMP, 1, P_SIZE), jnp.float32)], axis=2)
    scale = 1.0 / (COMP * NY * P_SIZE)
    applied = ((weight * sketched + flux - above) * scale).astype(jnp.bfloat16)
    rows = lax.dot_general(flat, applied.reshape(SKETCH, COMP * NY * P_SIZE), (((1,), (1,)), ((), ())), preferred_element_type=jnp.float32)
    core = jnp.dot(test.astype(jnp.float32).T, rows, precision=lax.Precision.HIGHEST) / SNAPS
    return rows.reshape(WRITERS, SNAPG, SKETCH), core
```

```python
import functools

import jax
import jax.numpy as jnp
import numpy as np
from jax import lax
from jax.experimental import pallas as pl
from jax.experimental.pallas import tpu as pltpu
from jax.sharding import PartitionSpec as P

MESH = pl.DeviceIdType.MESH
LANES = 128


def split3(value):
    high = value.astype(jnp.bfloat16)
    rest = value - high.astype(jnp.float32)
    mid = rest.astype(jnp.bfloat16)
    low = (rest - mid.astype(jnp.float32)).astype(jnp.bfloat16)
    return high, mid, low


def kernel(
    slabs,
    fields,
    snaps_ref,
    map_ref,
    omega_ref,
    level_ref,
    rows_ref,
    core_ref,
    x_ref,
    send_ref,
    recv_ref,
    wide_ref,
    xb_ref,
    vb_ref,
    coef_ref,
    part_ref,
    slab_ref,
    field_ref,
    full_ref,
    load_sem,
    send_sem,
    recv_sem,
    small_send,
    small_recv,
):
    devices = slabs * fields
    local, comps, planes, cells = x_ref.shape
    groups = LANES * devices // cells
    width = LANES // groups
    rows = planes // groups
    tiles = cells // LANES
    total = devices * local
    cols = omega_ref.shape[1]
    slab = lax.axis_index("slab")
    field = lax.axis_index("field")
    me = field * slabs + slab

    loads = [
        pltpu.make_async_copy(snaps_ref.at[0, :, a], x_ref.at[:, a], load_sem.at[a])
        for a in range(comps)
    ]
    for load in loads:
        load.start()

    barrier = pltpu.get_barrier_semaphore()

    def greet(k, carry):
        there = (me + k) % devices
        pl.semaphore_signal(
            barrier,
            inc=1,
            device_id={"slab": there % slabs, "field": there // slabs},
            device_id_type=MESH,
        )
        return carry

    lax.fori_loop(1, devices, greet, 0)

    def stage(a):
        for i in range(local):
            for t in range(tiles):
                parts = [
                    x_ref[i, a, g * rows : (g + 1) * rows, t * LANES : (t + 1) * LANES]
                    for g in range(groups)
                ]
                for q in range(groups):
                    send_ref[a, t * groups + q, i] = jnp.concatenate(
                        [p[:, q * width : (q + 1) * width] for p in parts], axis=1
                    )

    def send(a, ks, kf):
        to_slab = (slab + ks) % slabs
        to_field = (field + kf) % fields
        pltpu.make_async_remote_copy(
            src_ref=send_ref.at[a, to_field * slabs + to_slab],
            dst_ref=recv_ref.at[a, me],
            send_sem=send_sem.at[a],
            recv_sem=recv_sem.at[a],
            device_id={"slab": to_slab, "field": to_field},
            device_id_type=MESH,
        ).start()

    order = [k for k in (2, 1, 3, 0) if k < fields]

    def send_all(a):
        for kf in order:
            if kf:
                send(a, 0, kf)

        def step(ks, carry):
            for kf in order:
                send(a, ks, kf)
            return carry

        lax.fori_loop(1, slabs, step, 0)

    for a in range(comps):
        loads[a].wait()
        stage(a)
        recv_ref[a, me] = send_ref[a, me]
        if a == 0:
            pl.semaphore_wait(barrier, devices - 1)
        send_all(a)

    time = lax.broadcasted_iota(jnp.int32, (total, total), 0)
    onehot = (time == map_ref[...]).astype(jnp.float32).astype(jnp.bfloat16)
    omega = omega_ref[...].astype(jnp.float32).astype(jnp.bfloat16)
    test = lax.dot_general(
        onehot, omega, (((0,), (0,)), ((), ())), preferred_element_type=jnp.float32
    ).astype(jnp.bfloat16)
    test_t = lax.dot_general(
        omega, onehot, (((0,), (0,)), ((), ())), preferred_element_type=jnp.float32
    ).astype(jnp.bfloat16)

    scale = 1.0 / (comps * planes * cells)
    spacing = 0.5 * jnp.exp(level_ref[...].astype(jnp.float32) * np.float32(np.log(1.12)))
    inverse = 1.0 / spacing
    row_at = lax.broadcasted_iota(jnp.int32, (rows, planes), 0)
    plane_at = lax.broadcasted_iota(jnp.int32, (rows, planes), 1)
    lane_group = lax.broadcasted_iota(jnp.int32, (rows, LANES), 1) // width

    def pick(values, shift):
        out = jnp.zeros((rows, LANES), jnp.float32)
        for g in range(groups):
            hit = plane_at == row_at + (g * rows + shift)
            column = jnp.sum(jnp.where(hit, values, 0.0), axis=1, keepdims=True)
            out = jnp.where(lane_group == g, column, out)
        return out

    lower = pick(inverse, 0) * scale
    upper = pick(inverse, 1) * scale
    coef_ref[0] = pick(spacing, 0) * scale + lower + upper
    coef_ref[1] = lower
    coef_ref[2] = upper

    lane = lax.broadcasted_iota(jnp.int32, (total, LANES), 1)
    gram = None
    for a in range(comps):
        arrived = recv_ref.at[a, pl.ds(0, devices - 1)]
        pltpu.make_async_copy(arrived, arrived, recv_sem.at[a]).wait()

        def widen(d, carry):
            wide_ref[pl.ds(d * (local * rows), local * rows), :] = (
                recv_ref[a, d].reshape(local * rows, LANES).astype(jnp.float32)
            )
            return carry

        lax.fori_loop(0, devices, widen, 0, unroll=8)

        def load_row(j):
            return wide_ref[pl.ds(j, total, stride=rows), :]

        first = load_row(0)
        last = load_row(rows - 1)
        below = jnp.where(lane < width, 0.0, pltpu.roll(last, width, 1))
        here = first
        for j in range(rows):
            if j + 1 < rows:
                above = load_row(j + 1)
            else:
                above = jnp.where(
                    lane >= LANES - width, 0.0, pltpu.roll(first, LANES - width, 1)
                )
            applied = (
                coef_ref[0, j : j + 1, :] * here
                - coef_ref[1, j : j + 1, :] * below
                - coef_ref[2, j : j + 1, :] * above
            )
            xb_ref[:, j * LANES : (j + 1) * LANES] = here.astype(jnp.bfloat16)
            vb_ref[:, j * LANES : (j + 1) * LANES] = applied.astype(jnp.bfloat16)
            below, here = here, above
        term = lax.dot_general(
            xb_ref[...],
            vb_ref[...],
            (((1,), (1,)), ((), ())),
            preferred_element_type=jnp.float32,
        )
        gram = term if gram is None else gram + term

    pad = jnp.zeros((total, LANES - cols), jnp.float32)
    wide_test = jnp.concatenate([test.astype(jnp.float32), pad], axis=1).astype(jnp.bfloat16)
    partial = sum(
        jnp.dot(piece, wide_test, preferred_element_type=jnp.float32) for piece in split3(gram)
    )
    block = total // slabs
    part_ref[...] = partial.reshape(slabs, block, LANES)

    def small(src, dst, phase, to_slab, to_field):
        pltpu.make_async_remote_copy(
            src_ref=src,
            dst_ref=dst,
            send_sem=small_send.at[phase],
            recv_sem=small_recv.at[phase],
            device_id={"slab": to_slab, "field": to_field},
            device_id_type=MESH,
        ).start()

    def await_all(ref, count, phase):
        some = ref.at[pl.ds(0, count)]
        pltpu.make_async_copy(some, some, small_recv.at[phase]).wait()

    for ks in range(1, slabs):
        to = (slab + ks) % slabs
        small(part_ref.at[to], slab_ref.at[slab], 0, to, field)
    slab_ref[slab] = part_ref[slab]
    await_all(slab_ref, slabs - 1, 0)
    field_ref[field] = jnp.sum(slab_ref[...], axis=0)
    for kf in range(1, fields):
        small(field_ref.at[field], field_ref.at[field], 1, slab, (field + kf) % fields)
    await_all(field_ref, fields - 1, 1)
    full_ref[slab] = jnp.sum(field_ref[...], axis=0)
    for ks in range(1, slabs):
        small(full_ref.at[slab], full_ref.at[slab], 2, (slab + ks) % slabs, field)
    await_all(full_ref, slabs - 1, 2)

    blocks = slabs // fields
    own = full_ref[pl.ds(field * blocks, blocks)].reshape(total // fields, LANES)
    rows_ref[0] = own[:, :cols]
    sketch = full_ref[...].reshape(total, LANES)[:, :cols]
    core_ref[...] = (
        sum(jnp.dot(test_t, piece, preferred_element_type=jnp.float32) for piece in split3(sketch))
        / total
    )

    for a in range(comps):
        sent = send_ref.at[a, pl.ds(0, devices - 1)]
        pltpu.make_async_copy(sent, sent, send_sem.at[a]).wait()
    for phase, count in ((0, slabs - 1), (2, slabs - 1)):
        sent = slab_ref.at[pl.ds(0, count)]
        pltpu.make_async_copy(sent, sent, small_send.at[phase]).wait()
    sent = field_ref.at[pl.ds(0, fields - 1)]
    pltpu.make_async_copy(sent, sent, small_send.at[1]).wait()


def body(snaps, writer_map, omega, face_level):
    slabs = lax.axis_size("slab")
    fields = lax.axis_size("field")
    devices = slabs * fields
    _, local, comps, planes, cells = snaps.shape
    total, cols = omega.shape
    groups = LANES * devices // cells
    rows = planes // groups
    block = total // slabs
    chunk = (comps, devices, local, rows, LANES)
    vmem = pl.BlockSpec(memory_space=pltpu.VMEM)
    return pl.pallas_call(
        functools.partial(kernel, slabs, fields),
        out_shape=(
            jax.ShapeDtypeStruct((1, total // fields, cols), jnp.float32),
            jax.ShapeDtypeStruct((cols, cols), jnp.float32),
        ),
        in_specs=[pl.BlockSpec(memory_space=pl.ANY), vmem, vmem, vmem],
        out_specs=(vmem, vmem),
        scratch_shapes=[
            pltpu.VMEM((local, comps, planes, cells), jnp.bfloat16),
            pltpu.VMEM(chunk, jnp.bfloat16),
            pltpu.VMEM(chunk, jnp.bfloat16),
            pltpu.VMEM((total * rows, LANES), jnp.float32),
            pltpu.VMEM((total, rows * LANES), jnp.bfloat16),
            pltpu.VMEM((total, rows * LANES), jnp.bfloat16),
            pltpu.VMEM((3, rows, LANES), jnp.float32),
            pltpu.VMEM((slabs, block, LANES), jnp.float32),
            pltpu.VMEM((slabs, block, LANES), jnp.float32),
            pltpu.VMEM((fields, block, LANES), jnp.float32),
            pltpu.VMEM((slabs, block, LANES), jnp.float32),
            pltpu.SemaphoreType.DMA((comps,)),
            pltpu.SemaphoreType.DMA((comps,)),
            pltpu.SemaphoreType.DMA((comps,)),
            pltpu.SemaphoreType.DMA((3,)),
            pltpu.SemaphoreType.DMA((3,)),
        ],
        compiler_params=pltpu.CompilerParams(
            collective_id=0, has_side_effects=True, vmem_limit_bytes=40 * 1024 * 1024
        ),
    )(snaps, writer_map.reshape(1, total), omega, face_level.reshape(1, planes))


def solution(mesh):
    in_specs = (P("field", "slab", None, None, None), P(), P(), P())
    out_specs = (P("field", None, None), P())
    return jax.shard_map(body, mesh=mesh, in_specs=in_specs, out_specs=out_specs, check_vma=False)
```

```python
import functools

import jax
import jax.numpy as jnp
import numpy as np
from jax import lax
from jax.experimental import pallas as pl
from jax.experimental.pallas import tpu as pltpu
from jax.sharding import PartitionSpec as P

MESH = pl.DeviceIdType.MESH
LANES = 128


def split3(value):
    high = value.astype(jnp.bfloat16)
    rest = value - high.astype(jnp.float32)
    mid = rest.astype(jnp.bfloat16)
    low = (rest - mid.astype(jnp.float32)).astype(jnp.bfloat16)
    return high, mid, low


def kernel(
    slabs,
    fields,
    snaps_ref,
    map_hbm,
    omega_hbm,
    level_hbm,
    rows_ref,
    core_ref,
    x_ref,
    map_ref,
    omega_ref,
    level_ref,
    send_ref,
    recv_ref,
    wide_ref,
    xb_ref,
    vb_ref,
    coef_ref,
    part_ref,
    sum_ref,
    full_ref,
    load_sem,
    table_sem,
    send_sem,
    recv_sem,
    small_send,
    small_recv,
):
    devices = slabs * fields
    local, comps, planes, cells = x_ref.shape
    groups = LANES * devices // cells
    width = LANES // groups
    rows = planes // groups
    tiles = cells // LANES
    total = devices * local
    cols = omega_ref.shape[1]
    slab = lax.axis_index("slab")
    field = lax.axis_index("field")
    me = field * slabs + slab

    loads = [
        pltpu.make_async_copy(snaps_ref.at[0, :, a], x_ref.at[:, a], load_sem.at[a])
        for a in range(comps)
    ]
    tables = [
        pltpu.make_async_copy(src, dst, table_sem.at[n])
        for n, (src, dst) in enumerate(
            ((map_hbm, map_ref), (omega_hbm, omega_ref), (level_hbm, level_ref))
        )
    ]
    for load in loads + tables:
        load.start()

    barrier = pltpu.get_barrier_semaphore()

    def greet(k, carry):
        there = (me + k) % devices
        pl.semaphore_signal(
            barrier,
            inc=1,
            device_id={"slab": there % slabs, "field": there // slabs},
            device_id_type=MESH,
        )
        return carry

    lax.fori_loop(1, devices, greet, 0)

    def stage(a):
        for i in range(local):
            for t in range(tiles):
                parts = [
                    x_ref[i, a, g * rows : (g + 1) * rows, t * LANES : (t + 1) * LANES]
                    for g in range(groups)
                ]
                for q in range(groups):
                    send_ref[a, t * groups + q, i] = jnp.concatenate(
                        [p[:, q * width : (q + 1) * width] for p in parts], axis=1
                    )

    def send(a, ks, kf):
        to_slab = (slab + ks) % slabs
        to_field = (field + kf) % fields
        pltpu.make_async_remote_copy(
            src_ref=send_ref.at[a, to_field * slabs + to_slab],
            dst_ref=recv_ref.at[a, me],
            send_sem=send_sem.at[a],
            recv_sem=recv_sem.at[a],
            device_id={"slab": to_slab, "field": to_field},
            device_id_type=MESH,
        ).start()

    order = [k for k in (2, 1, 3, 0) if k < fields]

    def send_all(a):
        for kf in order:
            if kf:
                send(a, 0, kf)

        def step(ks, carry):
            for kf in order:
                send(a, ks, kf)
            return carry

        lax.fori_loop(1, slabs, step, 0)

    for a in range(comps):
        loads[a].wait()
        stage(a)
        recv_ref[a, me] = send_ref[a, me]
        if a == 0:
            pl.semaphore_wait(barrier, devices - 1)
        send_all(a)

    for table in tables:
        table.wait()

    time = lax.broadcasted_iota(jnp.int32, (total, total), 0)
    onehot = (time == map_ref[...]).astype(jnp.float32).astype(jnp.bfloat16)
    omega = omega_ref[...].astype(jnp.float32).astype(jnp.bfloat16)
    test = lax.dot_general(
        onehot, omega, (((0,), (0,)), ((), ())), preferred_element_type=jnp.float32
    ).astype(jnp.bfloat16)
    test_t = lax.dot_general(
        omega, onehot, (((0,), (0,)), ((), ())), preferred_element_type=jnp.float32
    ).astype(jnp.bfloat16)

    scale = 1.0 / (comps * planes * cells)
    spacing = 0.5 * jnp.exp(level_ref[...].astype(jnp.float32) * np.float32(np.log(1.12)))
    inverse = 1.0 / spacing
    row_at = lax.broadcasted_iota(jnp.int32, (rows, planes), 0)
    plane_at = lax.broadcasted_iota(jnp.int32, (rows, planes), 1)
    lane_group = lax.broadcasted_iota(jnp.int32, (rows, LANES), 1) // width

    def pick(values, shift):
        out = jnp.zeros((rows, LANES), jnp.float32)
        for g in range(groups):
            hit = plane_at == row_at + (g * rows + shift)
            column = jnp.sum(jnp.where(hit, values, 0.0), axis=1, keepdims=True)
            out = jnp.where(lane_group == g, column, out)
        return out

    lower = pick(inverse, 0) * scale
    upper = pick(inverse, 1) * scale
    coef_ref[0] = pick(spacing, 0) * scale + lower + upper
    coef_ref[1] = lower
    coef_ref[2] = upper

    lane = lax.broadcasted_iota(jnp.int32, (total, LANES), 1)
    gram = None
    for a in range(comps):
        arrived = recv_ref.at[a, pl.ds(0, devices - 1)]
        pltpu.make_async_copy(arrived, arrived, recv_sem.at[a]).wait()

        def widen(d, carry):
            wide_ref[pl.ds(d * (local * rows), local * rows), :] = (
                recv_ref[a, d].reshape(local * rows, LANES).astype(jnp.float32)
            )
            return carry

        lax.fori_loop(0, devices, widen, 0, unroll=8)

        def load_row(j):
            return wide_ref[pl.ds(j, total, stride=rows), :]

        first = load_row(0)
        last = load_row(rows - 1)
        below = jnp.where(lane < width, 0.0, pltpu.roll(last, width, 1))
        here = first
        for j in range(rows):
            if j + 1 < rows:
                above = load_row(j + 1)
            else:
                above = jnp.where(
                    lane >= LANES - width, 0.0, pltpu.roll(first, LANES - width, 1)
                )
            applied = (
                coef_ref[0, j : j + 1, :] * here
                - coef_ref[1, j : j + 1, :] * below
                - coef_ref[2, j : j + 1, :] * above
            )
            xb_ref[:, j * LANES : (j + 1) * LANES] = here.astype(jnp.bfloat16)
            vb_ref[:, j * LANES : (j + 1) * LANES] = applied.astype(jnp.bfloat16)
            below, here = here, above
        term = lax.dot_general(
            xb_ref[...],
            vb_ref[...],
            (((1,), (1,)), ((), ())),
            preferred_element_type=jnp.float32,
        )
        gram = term if gram is None else gram + term

    twice = jnp.concatenate([test.astype(jnp.float32)] * 2, axis=1).astype(jnp.bfloat16)
    partial = sum(
        jnp.dot(piece, twice, preferred_element_type=jnp.float32) for piece in split3(gram)
    )
    adders = slabs // 2
    half = total // slabs
    left = lax.broadcasted_iota(jnp.int32, (half, LANES), 1) < cols
    for b in range(adders):
        top = 2 * b * half
        part_ref[b] = jnp.where(
            left, partial[top : top + half], partial[top + half : top + 2 * half]
        )

    def small(src, dst, phase, to_slab, to_field):
        pltpu.make_async_remote_copy(
            src_ref=src,
            dst_ref=dst,
            send_sem=small_send.at[phase],
            recv_sem=small_recv.at[phase],
            device_id={"slab": to_slab, "field": to_field},
            device_id_type=MESH,
        ).start()

    def wait_blocks(ref, count, sem):
        some = ref.at[pl.ds(0, count)]
        pltpu.make_async_copy(some, some, sem).wait()

    mine = slab // 2
    adds = slab % 2 == 0
    for kf in order:
        for kb in range(adders):
            b = (mine + kb) % adders
            to_field = (field + kf) % fields
            if kf or kb:
                small(part_ref.at[b], sum_ref.at[me], 0, 2 * b, to_field)

    @pl.when(slab % 2 == 1)
    def _():
        small(part_ref.at[mine], sum_ref.at[me], 0, slab - 1, field)

    @pl.when(adds)
    def _():
        sum_ref[me] = part_ref[mine]
        wait_blocks(sum_ref, devices - 1, small_recv.at[0])
        full_ref[mine] = jnp.sum(sum_ref[...], axis=0)
        for ks in range(1, slabs):
            small(full_ref.at[mine], full_ref.at[mine], 1, (slab + ks) % slabs, field)
        wait_blocks(full_ref, adders - 1, small_recv.at[1])

    @pl.when(slab % 2 == 1)
    def _():
        wait_blocks(full_ref, adders, small_recv.at[1])

    def unpack(blocks, count):
        pieces = []
        for b in range(count):
            pieces += [blocks[b][:, :cols], blocks[b][:, cols : 2 * cols]]
        return jnp.concatenate(pieces, axis=0)

    held = adders // fields
    rows_ref[0] = unpack(full_ref[pl.ds(field * held, held)], held)
    sketch = unpack(full_ref[...], adders)
    core_ref[...] = (
        sum(jnp.dot(test_t, piece, preferred_element_type=jnp.float32) for piece in split3(sketch))
        / total
    )

    for a in range(comps):
        wait_blocks(send_ref.at[a], devices - 1, send_sem.at[a])
    wait_blocks(sum_ref, adders * fields - 1, small_send.at[0])

    @pl.when(slab % 2 == 1)
    def _():
        wait_blocks(sum_ref, 1, small_send.at[0])

    @pl.when(adds)
    def _():
        wait_blocks(sum_ref, slabs - 1, small_send.at[1])


def body(snaps, writer_map, omega, face_level):
    slabs = lax.axis_size("slab")
    fields = lax.axis_size("field")
    devices = slabs * fields
    _, local, comps, planes, cells = snaps.shape
    total, cols = omega.shape
    groups = LANES * devices // cells
    rows = planes // groups
    half = total // slabs
    chunk = (comps, devices, local, rows, LANES)
    vmem = pl.BlockSpec(memory_space=pltpu.VMEM)
    return pl.pallas_call(
        functools.partial(kernel, slabs, fields),
        out_shape=(
            jax.ShapeDtypeStruct((1, total // fields, cols), jnp.float32),
            jax.ShapeDtypeStruct((cols, cols), jnp.float32),
        ),
        in_specs=[pl.BlockSpec(memory_space=pltpu.HBM)] * 4,
        out_specs=(vmem, vmem),
        scratch_shapes=[
            pltpu.VMEM((local, comps, planes, cells), jnp.bfloat16),
            pltpu.VMEM((1, total), jnp.int32),
            pltpu.VMEM((total, cols), jnp.int32),
            pltpu.VMEM((1, planes), jnp.int32),
            pltpu.VMEM(chunk, jnp.bfloat16),
            pltpu.VMEM(chunk, jnp.bfloat16),
            pltpu.VMEM((total * rows, LANES), jnp.float32),
            pltpu.VMEM((total, rows * LANES), jnp.bfloat16),
            pltpu.VMEM((total, rows * LANES), jnp.bfloat16),
            pltpu.VMEM((3, rows, LANES), jnp.float32),
            pltpu.VMEM((slabs // 2, half, LANES), jnp.float32),
            pltpu.VMEM((devices, half, LANES), jnp.float32),
            pltpu.VMEM((slabs // 2, half, LANES), jnp.float32),
            pltpu.SemaphoreType.DMA((comps,)),
            pltpu.SemaphoreType.DMA((3,)),
            pltpu.SemaphoreType.DMA((comps,)),
            pltpu.SemaphoreType.DMA((comps,)),
            pltpu.SemaphoreType.DMA((2,)),
            pltpu.SemaphoreType.DMA((2,)),
        ],
        compiler_params=pltpu.CompilerParams(
            collective_id=0, has_side_effects=True, vmem_limit_bytes=60 * 1024 * 1024
        ),
    )(snaps, writer_map.reshape(1, total), omega, face_level.reshape(1, planes))


def solution(mesh):
    in_specs = (P("field", "slab", None, None, None), P(), P(), P())
    out_specs = (P("field", None, None), P())
    return jax.shard_map(body, mesh=mesh, in_specs=in_specs, out_specs=out_specs, check_vma=False)
```

```python
import functools

import jax
import jax.numpy as jnp
import numpy as np
from jax import lax
from jax.experimental import pallas as pl
from jax.experimental.pallas import tpu as pltpu
from jax.sharding import PartitionSpec as P

MESH = pl.DeviceIdType.MESH
LANES = 128


def split3(value):
    high = value.astype(jnp.bfloat16)
    rest = value - high.astype(jnp.float32)
    mid = rest.astype(jnp.bfloat16)
    low = (rest - mid.astype(jnp.float32)).astype(jnp.bfloat16)
    return high, mid, low


def kernel(
    slabs,
    fields,
    snaps_ref,
    map_hbm,
    omega_hbm,
    level_hbm,
    rows_ref,
    core_ref,
    x_ref,
    map_ref,
    omega_ref,
    level_ref,
    send_ref,
    recv_ref,
    wide_ref,
    xb_ref,
    vb_ref,
    coef_ref,
    part_ref,
    sum_ref,
    full_ref,
    load_sem,
    table_sem,
    send_sem,
    recv_sem,
    small_send,
    small_recv,
):
    devices = slabs * fields
    local, comps, planes, cells = x_ref.shape
    groups = LANES * devices // cells
    width = LANES // groups
    rows = planes // groups
    tiles = cells // LANES
    total = devices * local
    cols = omega_ref.shape[1]
    slab = lax.axis_index("slab")
    field = lax.axis_index("field")
    me = field * slabs + slab

    loads = [
        pltpu.make_async_copy(snaps_ref.at[0, :, a], x_ref.at[:, a], load_sem.at[a])
        for a in range(comps)
    ]
    tables = [
        pltpu.make_async_copy(src, dst, table_sem.at[n])
        for n, (src, dst) in enumerate(
            ((map_hbm, map_ref), (omega_hbm, omega_ref), (level_hbm, level_ref))
        )
    ]
    for load in loads + tables:
        load.start()

    barrier = pltpu.get_barrier_semaphore()

    def greet(k, carry):
        there = (me + k) % devices
        pl.semaphore_signal(
            barrier,
            inc=1,
            device_id={"slab": there % slabs, "field": there // slabs},
            device_id_type=MESH,
        )
        return carry

    lax.fori_loop(1, devices, greet, 0)

    def stage(a):
        for i in range(local):
            for t in range(tiles):
                parts = [
                    x_ref[i, a, g * rows : (g + 1) * rows, t * LANES : (t + 1) * LANES]
                    for g in range(groups)
                ]
                for q in range(groups):
                    send_ref[a, t * groups + q, i] = jnp.concatenate(
                        [p[:, q * width : (q + 1) * width] for p in parts], axis=1
                    )

    def send(a, ks, kf):
        to_slab = (slab + ks) % slabs
        to_field = (field + kf) % fields
        pltpu.make_async_remote_copy(
            src_ref=send_ref.at[a, to_field * slabs + to_slab],
            dst_ref=recv_ref.at[a, me],
            send_sem=send_sem.at[a],
            recv_sem=recv_sem.at[a],
            device_id={"slab": to_slab, "field": to_field},
            device_id_type=MESH,
        ).start()

    order = [k for k in (2, 1, 3, 0) if k < fields]

    def send_all(a):
        for kf in order:
            if kf:
                send(a, 0, kf)

        def step(ks, carry):
            for kf in order:
                send(a, ks, kf)
            return carry

        lax.fori_loop(1, slabs, step, 0)

    for a in range(comps):
        loads[a].wait()
        stage(a)
        recv_ref[a, me] = send_ref[a, me]
        if a == 0:
            pl.semaphore_wait(barrier, devices - 1)
        send_all(a)

    for table in tables:
        table.wait()

    time = lax.broadcasted_iota(jnp.int32, (total, total), 0)
    onehot = (time == map_ref[...]).astype(jnp.float32).astype(jnp.bfloat16)
    omega = omega_ref[...].astype(jnp.float32).astype(jnp.bfloat16)
    test = lax.dot_general(
        onehot, omega, (((0,), (0,)), ((), ())), preferred_element_type=jnp.float32
    ).astype(jnp.bfloat16)
    test_t = lax.dot_general(
        omega, onehot, (((0,), (0,)), ((), ())), preferred_element_type=jnp.float32
    ).astype(jnp.bfloat16)

    scale = 1.0 / (comps * planes * cells)
    spacing = 0.5 * jnp.exp(level_ref[...].astype(jnp.float32) * np.float32(np.log(1.12)))
    inverse = 1.0 / spacing
    row_at = lax.broadcasted_iota(jnp.int32, (rows, planes), 0)
    plane_at = lax.broadcasted_iota(jnp.int32, (rows, planes), 1)
    lane_group = lax.broadcasted_iota(jnp.int32, (rows, LANES), 1) // width

    def pick(values, shift):
        out = jnp.zeros((rows, LANES), jnp.float32)
        for g in range(groups):
            hit = plane_at == row_at + (g * rows + shift)
            column = jnp.sum(jnp.where(hit, values, 0.0), axis=1, keepdims=True)
            out = jnp.where(lane_group == g, column, out)
        return out

    lower = pick(inverse, 0) * scale
    upper = pick(inverse, 1) * scale
    coef_ref[0] = pick(spacing, 0) * scale + lower + upper
    coef_ref[1] = lower
    coef_ref[2] = upper

    lane = lax.broadcasted_iota(jnp.int32, (total, LANES), 1)
    gram = None
    for a in range(comps):
        arrived = recv_ref.at[a, pl.ds(0, devices - 1)]
        pltpu.make_async_copy(arrived, arrived, recv_sem.at[a]).wait()

        def widen(d, carry):
            wide_ref[pl.ds(d * (local * rows), local * rows), :] = (
                recv_ref[a, d].reshape(local * rows, LANES).astype(jnp.float32)
            )
            return carry

        lax.fori_loop(0, devices, widen, 0, unroll=8)

        def load_row(j):
            return wide_ref[pl.ds(j, total, stride=rows), :]

        first = load_row(0)
        last = load_row(rows - 1)
        below = jnp.where(lane < width, 0.0, pltpu.roll(last, width, 1))
        here = first
        for j in range(rows):
            if j + 1 < rows:
                above = load_row(j + 1)
            else:
                above = jnp.where(
                    lane >= LANES - width, 0.0, pltpu.roll(first, LANES - width, 1)
                )
            applied = (
                coef_ref[0, j : j + 1, :] * here
                - coef_ref[1, j : j + 1, :] * below
                - coef_ref[2, j : j + 1, :] * above
            )
            xb_ref[:, j * LANES : (j + 1) * LANES] = here.astype(jnp.bfloat16)
            vb_ref[:, j * LANES : (j + 1) * LANES] = applied.astype(jnp.bfloat16)
            below, here = here, above
        term = lax.dot_general(
            xb_ref[...],
            vb_ref[...],
            (((1,), (1,)), ((), ())),
            preferred_element_type=jnp.float32,
        )
        gram = term if gram is None else gram + term

    twice = jnp.concatenate([test.astype(jnp.float32)] * 2, axis=1).astype(jnp.bfloat16)
    partial = sum(
        jnp.dot(piece, twice, preferred_element_type=jnp.float32) for piece in split3(gram)
    )
    adders = slabs // 2
    half = total // slabs
    left = lax.broadcasted_iota(jnp.int32, (half, LANES), 1) < cols
    for b in range(adders):
        top = 2 * b * half
        part_ref[b] = jnp.where(
            left, partial[top : top + half], partial[top + half : top + 2 * half]
        )

    def small(src, dst, phase, to_slab, to_field):
        pltpu.make_async_remote_copy(
            src_ref=src,
            dst_ref=dst,
            send_sem=small_send.at[phase],
            recv_sem=small_recv.at[phase],
            device_id={"slab": to_slab, "field": to_field},
            device_id_type=MESH,
        ).start()

    def wait_blocks(ref, count, sem):
        some = ref.at[pl.ds(0, count)]
        pltpu.make_async_copy(some, some, sem).wait()

    mine = slab // 2
    adds = slab % 2 == 0
    for kf in order:
        for kb in range(adders):
            b = (mine + kb) % adders
            to_field = (field + kf) % fields
            if kf or kb:
                small(part_ref.at[b], sum_ref.at[me], 0, 2 * b, to_field)

    @pl.when(slab % 2 == 1)
    def _():
        small(part_ref.at[mine], sum_ref.at[me], 0, slab - 1, field)

    @pl.when(adds)
    def _():
        sum_ref[me] = part_ref[mine]
        wait_blocks(sum_ref, devices - 1, small_recv.at[0])
        full_ref[mine] = jnp.sum(sum_ref[...], axis=0)
        for ks in range(1, slabs):
            small(full_ref.at[mine], full_ref.at[mine], 1, (slab + ks) % slabs, field)
        wait_blocks(full_ref, adders - 1, small_recv.at[1])

    @pl.when(slab % 2 == 1)
    def _():
        wait_blocks(full_ref, adders, small_recv.at[1])

    def unpack(blocks, count):
        pieces = []
        for b in range(count):
            pieces += [blocks[b][:, :cols], blocks[b][:, cols : 2 * cols]]
        return jnp.concatenate(pieces, axis=0)

    held = adders // fields
    rows_ref[0] = unpack(full_ref[pl.ds(field * held, held)], held)
    sketch = unpack(full_ref[...], adders)
    core_ref[...] = (
        sum(jnp.dot(test_t, piece, preferred_element_type=jnp.float32) for piece in split3(sketch))
        / total
    )

    for a in range(comps):
        wait_blocks(send_ref.at[a], devices - 1, send_sem.at[a])
    wait_blocks(sum_ref, adders * fields - 1, small_send.at[0])

    @pl.when(slab % 2 == 1)
    def _():
        wait_blocks(sum_ref, 1, small_send.at[0])

    @pl.when(adds)
    def _():
        wait_blocks(sum_ref, slabs - 1, small_send.at[1])


def hand_on(rows_in, core_in, rows_out, core_out, sems):
    copies = [
        pltpu.make_async_copy(rows_in, rows_out, sems.at[0]),
        pltpu.make_async_copy(core_in, core_out, sems.at[1]),
    ]
    for copy in copies:
        copy.start()
    for copy in copies:
        copy.wait()


def body(snaps, writer_map, omega, face_level):
    slabs = lax.axis_size("slab")
    fields = lax.axis_size("field")
    devices = slabs * fields
    _, local, comps, planes, cells = snaps.shape
    total, cols = omega.shape
    groups = LANES * devices // cells
    rows = planes // groups
    half = total // slabs
    chunk = (comps, devices, local, rows, LANES)
    vmem = pl.BlockSpec(memory_space=pltpu.VMEM)
    hbm = pl.BlockSpec(memory_space=pltpu.HBM)
    out_shape = (
        jax.ShapeDtypeStruct((1, total // fields, cols), jnp.float32),
        jax.ShapeDtypeStruct((cols, cols), jnp.float32),
    )
    results = pl.pallas_call(
        functools.partial(kernel, slabs, fields),
        out_shape=out_shape,
        in_specs=[hbm] * 4,
        out_specs=(vmem, vmem),
        scratch_shapes=[
            pltpu.VMEM((local, comps, planes, cells), jnp.bfloat16),
            pltpu.VMEM((1, total), jnp.int32),
            pltpu.VMEM((total, cols), jnp.int32),
            pltpu.VMEM((1, planes), jnp.int32),
            pltpu.VMEM(chunk, jnp.bfloat16),
            pltpu.VMEM(chunk, jnp.bfloat16),
            pltpu.VMEM((total * rows, LANES), jnp.float32),
            pltpu.VMEM((total, rows * LANES), jnp.bfloat16),
            pltpu.VMEM((total, rows * LANES), jnp.bfloat16),
            pltpu.VMEM((3, rows, LANES), jnp.float32),
            pltpu.VMEM((slabs // 2, half, LANES), jnp.float32),
            pltpu.VMEM((devices, half, LANES), jnp.float32),
            pltpu.VMEM((slabs // 2, half, LANES), jnp.float32),
            pltpu.SemaphoreType.DMA((comps,)),
            pltpu.SemaphoreType.DMA((3,)),
            pltpu.SemaphoreType.DMA((comps,)),
            pltpu.SemaphoreType.DMA((comps,)),
            pltpu.SemaphoreType.DMA((2,)),
            pltpu.SemaphoreType.DMA((2,)),
        ],
        compiler_params=pltpu.CompilerParams(
            collective_id=0, has_side_effects=True, vmem_limit_bytes=60 * 1024 * 1024
        ),
    )(snaps, writer_map.reshape(1, total), omega, face_level.reshape(1, planes))
    return pl.pallas_call(
        hand_on,
        out_shape=out_shape,
        in_specs=[hbm] * 2,
        out_specs=(hbm, hbm),
        scratch_shapes=[pltpu.SemaphoreType.DMA((2,))],
        compiler_params=pltpu.CompilerParams(vmem_limit_bytes=60 * 1024 * 1024),
    )(*results)


def solution(mesh):
    in_specs = (P("field", "slab", None, None, None), P(), P(), P())
    out_specs = (P("field", None, None), P())
    return jax.shard_map(body, mesh=mesh, in_specs=in_specs, out_specs=out_specs, check_vma=False)
```

```python
import functools

import jax
import jax.numpy as jnp
import numpy as np
from jax import lax
from jax.experimental import pallas as pl
from jax.experimental.pallas import tpu as pltpu
from jax.sharding import PartitionSpec as P

MESH = pl.DeviceIdType.MESH
LANES = 128


def split3(value):
    high = value.astype(jnp.bfloat16)
    rest = value - high.astype(jnp.float32)
    mid = rest.astype(jnp.bfloat16)
    low = (rest - mid.astype(jnp.float32)).astype(jnp.bfloat16)
    return high, mid, low


def kernel(
    slabs,
    fields,
    snaps_ref,
    map_hbm,
    omega_hbm,
    level_hbm,
    rows_ref,
    core_ref,
    x_ref,
    map_ref,
    omega_ref,
    level_ref,
    send_ref,
    recv_ref,
    wide_ref,
    xb_ref,
    vb_ref,
    coef_ref,
    part_ref,
    sum_ref,
    full_ref,
    load_sem,
    table_sem,
    send_sem,
    recv_sem,
    small_send,
    small_recv,
):
    devices = slabs * fields
    local, comps, planes, cells = x_ref.shape
    groups = LANES * devices // cells
    width = LANES // groups
    rows = planes // groups
    tiles = cells // LANES
    total = devices * local
    cols = omega_ref.shape[1]
    slab = lax.axis_index("slab")
    field = lax.axis_index("field")
    me = field * slabs + slab

    loads = [
        pltpu.make_async_copy(snaps_ref.at[0, :, a], x_ref.at[:, a], load_sem.at[a])
        for a in range(comps)
    ]
    tables = [
        pltpu.make_async_copy(src, dst, table_sem.at[n])
        for n, (src, dst) in enumerate(
            ((map_hbm, map_ref), (omega_hbm, omega_ref), (level_hbm, level_ref))
        )
    ]
    for load in loads + tables:
        load.start()

    barrier = pltpu.get_barrier_semaphore()

    def greet(k, carry):
        there = (me + k) % devices
        pl.semaphore_signal(
            barrier,
            inc=1,
            device_id={"slab": there % slabs, "field": there // slabs},
            device_id_type=MESH,
        )
        return carry

    lax.fori_loop(1, devices, greet, 0)

    def stage(a):
        for i in range(local):
            for t in range(tiles):
                parts = [
                    x_ref[i, a, g * rows : (g + 1) * rows, t * LANES : (t + 1) * LANES]
                    for g in range(groups)
                ]
                for q in range(groups):
                    send_ref[a, t * groups + q, i] = jnp.concatenate(
                        [p[:, q * width : (q + 1) * width] for p in parts], axis=1
                    )

    def send(a, ks, kf):
        to_slab = (slab + ks) % slabs
        to_field = (field + kf) % fields
        pltpu.make_async_remote_copy(
            src_ref=send_ref.at[a, to_field * slabs + to_slab],
            dst_ref=recv_ref.at[a, me],
            send_sem=send_sem.at[a],
            recv_sem=recv_sem.at[a],
            device_id={"slab": to_slab, "field": to_field},
            device_id_type=MESH,
        ).start()

    order = [k for k in (2, 1, 3, 0) if k < fields]

    def send_all(a):
        for kf in order:
            if kf:
                send(a, 0, kf)

        def step(ks, carry):
            for kf in order:
                send(a, ks, kf)
            return carry

        lax.fori_loop(1, slabs, step, 0)

    for a in range(comps):
        loads[a].wait()
        stage(a)
        recv_ref[a, me] = send_ref[a, me]
        if a == 0:
            pl.semaphore_wait(barrier, devices - 1)
        send_all(a)

    for table in tables:
        table.wait()

    time = lax.broadcasted_iota(jnp.int32, (total, total), 0)
    onehot = (time == map_ref[...]).astype(jnp.float32).astype(jnp.bfloat16)
    omega = omega_ref[...].astype(jnp.float32).astype(jnp.bfloat16)
    test = lax.dot_general(
        onehot, omega, (((0,), (0,)), ((), ())), preferred_element_type=jnp.float32
    ).astype(jnp.bfloat16)
    test_t = lax.dot_general(
        omega, onehot, (((0,), (0,)), ((), ())), preferred_element_type=jnp.float32
    ).astype(jnp.bfloat16)

    scale = 1.0 / (comps * planes * cells)
    spacing = 0.5 * jnp.exp(level_ref[...].astype(jnp.float32) * np.float32(np.log(1.12)))
    inverse = 1.0 / spacing
    row_at = lax.broadcasted_iota(jnp.int32, (rows, planes), 0)
    plane_at = lax.broadcasted_iota(jnp.int32, (rows, planes), 1)
    lane_group = lax.broadcasted_iota(jnp.int32, (rows, LANES), 1) // width

    def pick(values, shift):
        out = jnp.zeros((rows, LANES), jnp.float32)
        for g in range(groups):
            hit = plane_at == row_at + (g * rows + shift)
            column = jnp.sum(jnp.where(hit, values, 0.0), axis=1, keepdims=True)
            out = jnp.where(lane_group == g, column, out)
        return out

    lower = pick(inverse, 0) * scale
    upper = pick(inverse, 1) * scale
    coef_ref[0] = pick(spacing, 0) * scale + lower + upper
    coef_ref[1] = lower
    coef_ref[2] = upper

    lane = lax.broadcasted_iota(jnp.int32, (total, LANES), 1)
    gram = None
    for a in range(comps):
        arrived = recv_ref.at[a, pl.ds(0, devices - 1)]
        pltpu.make_async_copy(arrived, arrived, recv_sem.at[a]).wait()

        def widen(d, carry):
            wide_ref[pl.ds(d * (local * rows), local * rows), :] = (
                recv_ref[a, d].reshape(local * rows, LANES).astype(jnp.float32)
            )
            return carry

        lax.fori_loop(0, devices, widen, 0, unroll=8)

        def load_row(j):
            return wide_ref[pl.ds(j, total, stride=rows), :]

        first = load_row(0)
        last = load_row(rows - 1)
        below = jnp.where(lane < width, 0.0, pltpu.roll(last, width, 1))
        here = first
        for j in range(rows):
            if j + 1 < rows:
                above = load_row(j + 1)
            else:
                above = jnp.where(
                    lane >= LANES - width, 0.0, pltpu.roll(first, LANES - width, 1)
                )
            applied = (
                coef_ref[0, j : j + 1, :] * here
                - coef_ref[1, j : j + 1, :] * below
                - coef_ref[2, j : j + 1, :] * above
            )
            xb_ref[:, j * LANES : (j + 1) * LANES] = here.astype(jnp.bfloat16)
            vb_ref[:, j * LANES : (j + 1) * LANES] = applied.astype(jnp.bfloat16)
            below, here = here, above
        term = lax.dot_general(
            xb_ref[...],
            vb_ref[...],
            (((1,), (1,)), ((), ())),
            preferred_element_type=jnp.float32,
        )
        gram = term if gram is None else gram + term

    twice = jnp.concatenate([test.astype(jnp.float32)] * 2, axis=1).astype(jnp.bfloat16)
    partial = sum(
        jnp.dot(piece, twice, preferred_element_type=jnp.float32) for piece in split3(gram)
    )
    adders = slabs // 2
    half = total // slabs
    left = lax.broadcasted_iota(jnp.int32, (half, LANES), 1) < cols
    for b in range(adders):
        top = 2 * b * half
        part_ref[b] = jnp.where(
            left, partial[top : top + half], partial[top + half : top + 2 * half]
        )

    def small(src, dst, phase, to_slab, to_field):
        pltpu.make_async_remote_copy(
            src_ref=src,
            dst_ref=dst,
            send_sem=small_send.at[phase],
            recv_sem=small_recv.at[phase],
            device_id={"slab": to_slab, "field": to_field},
            device_id_type=MESH,
        ).start()

    def wait_blocks(ref, count, sem):
        some = ref.at[pl.ds(0, count)]
        pltpu.make_async_copy(some, some, sem).wait()

    mine = slab // 2
    adds = slab % 2 == 0
    for kf in order:
        for kb in range(adders):
            b = (mine + kb) % adders
            to_field = (field + kf) % fields
            if kf or kb:
                small(part_ref.at[b], sum_ref.at[me], 0, 2 * b, to_field)

    @pl.when(slab % 2 == 1)
    def _():
        small(part_ref.at[mine], sum_ref.at[me], 0, slab - 1, field)

    @pl.when(adds)
    def _():
        sum_ref[me] = part_ref[mine]
        wait_blocks(sum_ref, devices - 1, small_recv.at[0])
        full_ref[mine] = jnp.sum(sum_ref[...], axis=0)
        for ks in range(1, slabs):
            small(full_ref.at[mine], full_ref.at[mine], 1, (slab + ks) % slabs, field)
        wait_blocks(full_ref, adders - 1, small_recv.at[1])

    @pl.when(slab % 2 == 1)
    def _():
        wait_blocks(full_ref, adders, small_recv.at[1])

    def unpack(blocks, count):
        pieces = []
        for b in range(count):
            pieces += [blocks[b][:, :cols], blocks[b][:, cols : 2 * cols]]
        return jnp.concatenate(pieces, axis=0)

    held = adders // fields
    rows_ref[0] = unpack(full_ref[pl.ds(field * held, held)], held)
    sketch = unpack(full_ref[...], adders)
    core_ref[...] = (
        sum(jnp.dot(test_t, piece, preferred_element_type=jnp.float32) for piece in split3(sketch))
        / total
    )

    for a in range(comps):
        wait_blocks(send_ref.at[a], devices - 1, send_sem.at[a])
    wait_blocks(sum_ref, adders * fields - 1, small_send.at[0])

    @pl.when(slab % 2 == 1)
    def _():
        wait_blocks(sum_ref, 1, small_send.at[0])

    @pl.when(adds)
    def _():
        wait_blocks(sum_ref, slabs - 1, small_send.at[1])


def hand_on(rows_in, core_in, rows_out, core_out, rows_held, core_held, in_sems, out_sems):
    steps = ((rows_in, rows_held, rows_out), (core_in, core_held, core_out))
    loads = [pltpu.make_async_copy(a, b, in_sems.at[n]) for n, (a, b, c) in enumerate(steps)]
    stores = [pltpu.make_async_copy(b, c, out_sems.at[n]) for n, (a, b, c) in enumerate(steps)]
    for load in loads:
        load.start()
    for load, store in zip(loads, stores):
        load.wait()
        store.start()
    for store in stores:
        store.wait()


def body(snaps, writer_map, omega, face_level):
    slabs = lax.axis_size("slab")
    fields = lax.axis_size("field")
    devices = slabs * fields
    _, local, comps, planes, cells = snaps.shape
    total, cols = omega.shape
    groups = LANES * devices // cells
    rows = planes // groups
    half = total // slabs
    chunk = (comps, devices, local, rows, LANES)
    vmem = pl.BlockSpec(memory_space=pltpu.VMEM)
    hbm = pl.BlockSpec(memory_space=pltpu.HBM)
    out_shape = (
        jax.ShapeDtypeStruct((1, total // fields, cols), jnp.float32),
        jax.ShapeDtypeStruct((cols, cols), jnp.float32),
    )
    results = pl.pallas_call(
        functools.partial(kernel, slabs, fields),
        out_shape=out_shape,
        in_specs=[hbm] * 4,
        out_specs=(vmem, vmem),
        scratch_shapes=[
            pltpu.VMEM((local, comps, planes, cells), jnp.bfloat16),
            pltpu.VMEM((1, total), jnp.int32),
            pltpu.VMEM((total, cols), jnp.int32),
            pltpu.VMEM((1, planes), jnp.int32),
            pltpu.VMEM(chunk, jnp.bfloat16),
            pltpu.VMEM(chunk, jnp.bfloat16),
            pltpu.VMEM((total * rows, LANES), jnp.float32),
            pltpu.VMEM((total, rows * LANES), jnp.bfloat16),
            pltpu.VMEM((total, rows * LANES), jnp.bfloat16),
            pltpu.VMEM((3, rows, LANES), jnp.float32),
            pltpu.VMEM((slabs // 2, half, LANES), jnp.float32),
            pltpu.VMEM((devices, half, LANES), jnp.float32),
            pltpu.VMEM((slabs // 2, half, LANES), jnp.float32),
            pltpu.SemaphoreType.DMA((comps,)),
            pltpu.SemaphoreType.DMA((3,)),
            pltpu.SemaphoreType.DMA((comps,)),
            pltpu.SemaphoreType.DMA((comps,)),
            pltpu.SemaphoreType.DMA((2,)),
            pltpu.SemaphoreType.DMA((2,)),
        ],
        compiler_params=pltpu.CompilerParams(
            collective_id=0, has_side_effects=True, vmem_limit_bytes=60 * 1024 * 1024
        ),
    )(snaps, writer_map.reshape(1, total), omega, face_level.reshape(1, planes))
    return pl.pallas_call(
        hand_on,
        out_shape=out_shape,
        in_specs=[hbm] * 2,
        out_specs=(hbm, hbm),
        scratch_shapes=[
            pltpu.VMEM(out_shape[0].shape, jnp.float32),
            pltpu.VMEM(out_shape[1].shape, jnp.float32),
            pltpu.SemaphoreType.DMA((2,)),
            pltpu.SemaphoreType.DMA((2,)),
        ],
        compiler_params=pltpu.CompilerParams(vmem_limit_bytes=60 * 1024 * 1024),
    )(*results)


def solution(mesh):
    in_specs = (P("field", "slab", None, None, None), P(), P(), P())
    out_specs = (P("field", None, None), P())
    return jax.shard_map(body, mesh=mesh, in_specs=in_specs, out_specs=out_specs, check_vma=False)
```
